32 devices in a mesh: head: 4 (over x, core), ctx: 8 (over z, y).
Axes of the slice: x: 2, y: 2, z: 4, core: 2. Of those that a mesh axis runs over, the one named last changes fastest.
Arguments:
- query_rows: bfloat16 [3072, 16, 128], P(('ctx', 'head')), may hold values from -1.6953125 to 1.6953125
- key_matrix: bfloat16 [3072, 1, 128], P(('ctx', 'head')), may hold values from -1.6953125 to 1.6953125
- value_matrix: bfloat16 [3072, 1, 128], P(('ctx', 'head')), may hold values from -6 to 6
- output_rows: bfloat16 [3072, 16, 128], P(('ctx', 'head')), may hold values from -3 to 3
- out_grad: bfloat16 [3072, 16, 128], P(('ctx', 'head')), may hold values from -6 to 6
- log_norm: float32 [3072, 16], P(('ctx', 'head')), as said below
- span_order: int32 [16], replicated, may hold values from 0 to 15, as said below
Outputs:
- query_grad: bfloat16 [3072, 16, 128], P(('ctx', 'head'))
- key_grad: bfloat16 [3072, 1, 128], P(('ctx', 'head'))
- value_grad: bfloat16 [3072, 1, 128], P(('ctx', 'head'))
The draws below stay inside these ranges and needn't reach their ends.
Inputs may be any that keep to these rules, and one draw needn't show every extreme that they name: A permutation of 0 to 15: stored span j of every token-indexed array holds the tokens of sequence span span_order[j]. `log_norm`: the normalizers of the forward pass in the log domain, of the size of the logarithm of the row's position in the sequence.
All inputs are finite; a program needn't handle non-finite values.
Results may differ from the reference program's by a relative error of at most 0.0051.
Values may be sent and summed in bfloat16 or wider, within the bound.
A program may use at most 64 MiB of HBM per device.

```python
import jax
import jax.numpy as jnp
from jax import lax

HEAD_DIMENSION = 128
HQ = 16
SHARD_KEY_HEADS = 1
SPAN = 192
SPANS = 16
TOKEN_COUNT = 3072


def span_permutation(key):
    return jax.random.permutation(jax.random.fold_in(key, 11), SPANS).astype(jnp.int32)


def draw_span_order(key, part):
    return span_permutation(key)


def draw_log_norm(key, part):
    span_perm = span_permutation(key)
    row_ids = jnp.arange(TOKEN_COUNT, dtype=jnp.int32)
    place = span_perm[row_ids // SPAN] * SPAN + row_ids % SPAN
    baseline = jnp.log(place.astype(jnp.float32) + 1.0) + 0.5
    noise_key = jax.random.fold_in(key, 23)
    spread = jax.random.uniform(noise_key, (TOKEN_COUNT, HQ), jnp.float32, -0.5, 0.5)
    return baseline[:, None] + spread


def block_scale(own_key, extent, cuts, smallest, top_value):
    level, own = 1.0, jax.random.fold_in(own_key, 6)
    for axis_at, shards_of in cuts:
        steps = jnp.exp(jax.random.uniform(jax.random.fold_in(own, axis_at), (shards_of,), jnp.float32, smallest / len(cuts), top_value / len(cuts)))
        level = level * jnp.repeat(steps, extent[axis_at] // shards_of).reshape([-1 if axis == axis_at else 1 for axis in range(len(extent))])
    return level


def bell_draw(own_key, shape, scale, limit, shards=(), kind=jnp.bfloat16):
    loudness = block_scale(own_key, shape, shards, -0.22, 0.18) if shards else 1.0
    result = jax.random.normal(own_key, shape, jnp.float32) * scale * loudness
    return jnp.minimum(jnp.maximum(result, -limit), limit).astype(kind)


def setup_inputs(seed: int = 0) -> dict:
    arg_keys = jax.random.split(jax.random.key(seed), 8)
    return {
        "query_rows": jnp.clip(jax.random.uniform(arg_keys[0], (TOKEN_COUNT, HQ, HEAD_DIMENSION), jnp.float32, -1.6953125, 1.6953125) * block_scale(arg_keys[0], (TOKEN_COUNT, HQ, HEAD_DIMENSION), ((0, 32),), -0.4, 0.0), -1.6953125, 1.6953125).astype(jnp.bfloat16),
        "key_matrix": jnp.clip(jax.random.uniform(arg_keys[1], (TOKEN_COUNT, SHARD_KEY_HEADS, HEAD_DIMENSION), jnp.float32, -1.6953125, 1.6953125) * block_scale(arg_keys[1], (TOKEN_COUNT, SHARD_KEY_HEADS, HEAD_DIMENSION), ((0, 32),), -0.4, 0.0), -1.6953125, 1.6953125).astype(jnp.bfloat16),
        "value_matrix": bell_draw(arg_keys[2], (TOKEN_COUNT, SHARD_KEY_HEADS, HEAD_DIMENSION), 1.0, 6.0, ((0, 32),)),
        "output_rows": bell_draw(arg_keys[3], (TOKEN_COUNT, HQ, HEAD_DIMENSION), 0.5, 3.0, ((0, 32),)),
        "out_grad": bell_draw(arg_keys[4], (TOKEN_COUNT, HQ, HEAD_DIMENSION), 1.0, 6.0, ((0, 32),)),
        "log_norm": draw_log_norm(jax.random.fold_in(arg_keys[7], 71), 0),
        "span_order": draw_span_order(jax.random.fold_in(arg_keys[7], 71), 0),
    }


def block_grads(queries, grads_out, lse_rows, delta_rows, key_matrix, value_matrix, allowed, scale):
    f32 = jnp.float32
    hi = lax.Precision.HIGHEST
    logit_scores = jnp.einsum("qhd,kd->qhk", queries, key_matrix, precision=hi) * scale
    shifted = jnp.where(allowed[:, None, :], logit_scores - lse_rows[:, :, None], -jnp.inf)
    soft_probs = jnp.exp(shifted)
    probs_b = lax.optimization_barrier(soft_probs.astype(jnp.bfloat16)).astype(f32)
    value_part = jnp.einsum("qhk,qhd->kd", probs_b, grads_out, precision=hi)
    prob_grads = jnp.einsum("qhd,kd->qhk", grads_out, value_matrix, precision=hi)
    score_grads = lax.optimization_barrier((soft_probs * (prob_grads - delta_rows[:, :, None])).astype(jnp.bfloat16)).astype(f32)
    query_part = jnp.einsum("qhk,kd->qhd", score_grads, key_matrix, precision=hi)
    key_part = jnp.einsum("qhk,qhd->kd", score_grads, queries, precision=hi)
    return query_part, key_part, value_part


def reference(query_rows, key_matrix, value_matrix, output_rows, out_grad, log_norm, span_order):
    f32 = jnp.float32
    seq_len = query_rows.shape[0]
    span_count = span_order.shape[0]
    span_len = seq_len // span_count
    head_q = query_rows.shape[1]
    head_kv = key_matrix.shape[1]
    head_size = query_rows.shape[2]
    group = head_q // head_kv
    scale = head_size ** -0.5
    row_ids = jnp.arange(seq_len, dtype=jnp.int32)
    stored_pos = span_order[row_ids // span_len] * span_len + row_ids % span_len
    inverse = jnp.zeros((span_count,), jnp.int32).at[span_order].set(jnp.arange(span_count, dtype=jnp.int32))
    seq_rows = inverse[row_ids // span_len] * span_len + row_ids % span_len
    queries = query_rows[seq_rows].astype(f32)
    key_seq = key_matrix[seq_rows].astype(f32)
    value_seq = value_matrix[seq_rows].astype(f32)
    grads_out = out_grad[seq_rows].astype(f32)
    outputs = output_rows[seq_rows].astype(f32)
    lse_seq = log_norm[seq_rows].astype(f32)
    delta = jnp.sum(grads_out * outputs, axis=-1)
    block_len = span_len
    block_count = span_count
    query_sum = jnp.zeros((seq_len, head_q, head_size), f32)
    key_sum = jnp.zeros((seq_len, head_kv, head_size), f32)
    value_sum = jnp.zeros((seq_len, head_kv, head_size), f32)
    for query_group_index in range(head_kv):
        first = query_group_index * group
        for block_index in range(block_count):
            low = block_index * block_len
            high = low + block_len
            allowed = jnp.arange(high, dtype=jnp.int32)[None, :] <= jnp.arange(low, high, dtype=jnp.int32)[:, None]
            query_part, key_part, value_part = block_grads(
                queries[low:high, first:first + group], grads_out[low:high, first:first + group],
                lse_seq[low:high, first:first + group], delta[low:high, first:first + group],
                key_seq[:high, query_group_index], value_seq[:high, query_group_index], allowed, scale)
            query_sum = query_sum.at[low:high, first:first + group].set(query_part)
            key_sum = key_sum.at[:high, query_group_index].add(key_part)
            value_sum = value_sum.at[:high, query_group_index].add(value_part)
    query_grad = (query_sum * scale).astype(jnp.bfloat16)[stored_pos]
    key_grad = (key_sum * scale).astype(jnp.bfloat16)[stored_pos]
    value_grad = value_sum.astype(jnp.bfloat16)[stored_pos]
    return (query_grad, key_grad, value_grad)
```

```python
import functools

import jax
import jax.numpy as jnp
from jax import lax
from jax.experimental import pallas as pl
from jax.experimental.pallas import tpu as pltpu
from jax.sharding import PartitionSpec as P

MESH = pl.DeviceIdType.MESH
LOG2E = 1.4426950408889634
BIG = 1e30


def dot(a, b, ca, cb):
    return lax.dot_general(a, b, (((ca,), (cb,)), ((), ())), preferred_element_type=jnp.float32)


def chunk_size(rows, keys):
    chunk = 512 if keys <= 512 else 128
    while rows % chunk:
        chunk //= 2
    return chunk


def kernel(nz, span_ref, q_ref, k_ref, v_ref, o_ref, do_ref, lse_ref, dq_ref, dk_ref, dv_ref,
           kv, pq, pdo, stats, pstats, kt, acc, acc0, dqt, dqt_p, dq_out, dq_in,
           part_out, part_in, line_out, line_in,
           x_send, x_recv, z_send, z_recv, p_send, p_recv, q_send, q_recv,
           r_send, r_recv, l_send, l_recv):
    f32, bf16 = jnp.float32, jnp.bfloat16
    t = k_ref.shape[0]
    head_size = k_ref.shape[1]
    rows = q_ref.shape[0]
    heads = rows // t
    keys = nz * t
    scale = head_size ** -0.5
    c = lax.axis_index("ctx")
    h = lax.axis_index("head")
    core = lax.rem(h, 2)
    x = lax.div(h, 2)
    y = lax.rem(c, 2)
    z = lax.div(c, 2)

    partner = {"ctx": c, "head": x * 2 + (1 - core)}

    def plane(q):
        xx = 1 - x if q % 2 else x
        yy = 1 - y if q // 2 else y
        return xx, yy

    def plane_id(q):
        xx, yy = plane(q)
        return {"ctx": z * 2 + yy, "head": xx * 2 + core}

    def line_id(d):
        return {"ctx": lax.rem(z + d, nz) * 2 + y, "head": h}

    barrier = pltpu.get_barrier_semaphore()
    peers = [partner] + [plane_id(q) for q in (1, 2, 3)] + [line_id(d) for d in range(1, nz)]
    for peer in peers:
        pl.semaphore_signal(barrier, inc=1, device_id=peer, device_id_type=MESH)

    kv[0, 0, 0] = k_ref[...]
    kv[0, 0, 1] = v_ref[...]

    prod = o_ref[...].astype(f32) * do_ref[...].astype(f32)
    prod_hi = prod.astype(bf16)
    prod_lo = (prod - prod_hi.astype(f32)).astype(bf16)
    ones = jnp.ones((8, head_size), bf16)
    delta = dot(ones, prod_hi, 1, 1) + dot(ones, prod_lo, 1, 1)
    stats[0:1, :] = lse_ref[...] * LOG2E
    stats[1:2, :] = delta[0:1, :]

    pl.semaphore_wait(barrier, len(peers))

    def remote(src, dst, ss, rs, dev):
        return pltpu.make_async_remote_copy(
            src_ref=src, dst_ref=dst, send_sem=ss, recv_sem=rs, device_id=dev, device_id_type=MESH)

    zc = [None] + [remote(kv.at[0, 0], kv.at[0, nz - d], z_send.at[d], z_recv.at[nz - d], line_id(d))
                   for d in range(1, nz)]
    pc = {(q, d): remote(kv.at[0, d], kv.at[q, d], p_send.at[q, d], p_recv.at[q, d], plane_id(q))
          for q in (1, 2, 3) for d in range(nz)}
    xc = [remote(q_ref, pq, x_send.at[0], x_recv.at[0], partner),
          remote(do_ref, pdo, x_send.at[1], x_recv.at[1], partner),
          remote(stats, pstats, x_send.at[2], x_recv.at[2], partner)]
    for d in range(1, nz):
        zc[d].start()
    for q in (1, 2, 3):
        pc[q, 0].start()
    xc[2].start()
    xc[0].start()
    xc[1].start()

    def z_arrival(d):
        return remote(kv.at[0, 0], kv.at[0, d], z_send.at[nz - d], z_recv.at[d], line_id(nz - d))

    for d in sorted(range(1, nz), key=lambda d: min(d, nz - d)):
        z_arrival(d).wait_recv()
        for q in (1, 2, 3):
            pc[q, d].start()

    own_span = c * (lax.axis_size("head") // 2) + x
    own_place = span_ref[own_span]
    chunk = chunk_size(rows, keys)

    def prepare(q):
        block = kv[q, :, 0].reshape(keys, head_size)
        kt[...] = block.astype(f32).T.astype(bf16)

    def work(q, row_q, row_do, row_stats, row_core, dq_acc, first, total, total_first):
        xx, yy = plane(q)
        lifts = []
        for d in range(nz):
            zz = lax.rem(z + d, nz)
            place = span_ref[(zz * 2 + yy) * (lax.axis_size("head") // 2) + xx]
            lifts.append(jnp.where(place > own_place, jnp.float32(BIG), jnp.float32(0.0)))
        if total_first:
            total[...] = jnp.zeros(total.shape, f32)

        def body(i, carry):
            low = pl.multiple_of(i * chunk, chunk)
            at = pl.ds(low, chunk)
            qs = row_q[at, :]
            gs = row_do[at, :]
            lse = row_stats[0:1, at]
            delt = row_stats[1:2, at]
            kb = kv[q, :, 0].reshape(keys, head_size)
            vb = kv[q, :, 1].reshape(keys, head_size)
            s = dot(kb, qs, 1, 1)
            dp = dot(vb, gs, 1, 1)
            ps, dss = [], []
            for d in range(nz):
                part = slice(d * t, (d + 1) * t)
                e = s[part] * (scale * LOG2E) - (lse + lifts[d])
                if q == 0 and d == 0:
                    key_at = lax.broadcasted_iota(jnp.int32, (t, chunk), 0) + core * t
                    row_at = lax.broadcasted_iota(jnp.int32, (t, chunk), 1) + low
                    row_at = lax.div(row_at, heads) + row_core * t
                    e = jnp.where(key_at <= row_at, e, -BIG)
                p = jnp.exp2(e)
                ps.append(p.astype(bf16))
                dss.append((p * (dp[part] - delt)).astype(bf16))
            p = jnp.concatenate(ps, axis=0)
            ds = jnp.concatenate(dss, axis=0)
            total[0] += dot(ds, qs, 1, 0)
            total[1] += dot(p, gs, 1, 0)
            dqt = dot(kt[...], ds, 1, 0)
            if first:
                dq_acc[:, at] = dqt
            else:
                dq_acc[:, at] += dqt
            return carry

        lax.fori_loop(0, rows // chunk, body, 0)

    for copy in xc:
        copy.wait_recv()
    prepare(0)
    work(0, pq, pdo, pstats, 1 - core, dqt_p, True, acc0, True)
    rc = {}
    for q in (1, 2, 3):
        for d in range(nz):
            pc[q, d].wait_recv()
        prepare(q)
        work(q, pq, pdo, pstats, 1 - core, dqt_p, False, acc, True)
        work(q, q_ref, do_ref, stats, core, dqt, q == 1, acc, False)
        for d in range(nz):
            part_out[q - 1, d] = acc[:, d * t:(d + 1) * t, :].astype(bf16)
        rc[q] = remote(part_out.at[q - 1], part_in.at[q - 1], r_send.at[q - 1], r_recv.at[q - 1], plane_id(q))
        rc[q].start()
    dq_out[...] = dqt_p[...].T.astype(bf16)
    qc = remote(dq_out, dq_in, q_send, q_recv, partner)
    qc.start()
    prepare(0)
    work(0, q_ref, do_ref, stats, core, dqt, False, acc0, False)
    for q in (1, 2, 3):
        rc[q].wait_recv()

    def plane_sum(d):
        value = acc0[:, d * t:(d + 1) * t, :]
        for q in (1, 2, 3):
            value = value + part_in[q - 1, d].astype(f32)
        return value

    lc = [None]
    for d in range(1, nz):
        line_out[d - 1] = plane_sum(d).astype(bf16)
        lc.append(remote(line_out.at[d - 1], line_in.at[nz - d - 1], l_send.at[d - 1],
                         l_recv.at[nz - d - 1], line_id(d)))
        lc[d].start()
    own = plane_sum(0)
    qc.wait_recv()
    dq_ref[...] = ((dqt[...].T + dq_in[...].astype(f32)) * scale).astype(bf16)
    for d in range(1, nz):
        remote(line_out.at[nz - d - 1], line_in.at[d - 1], l_send.at[nz - d - 1],
               l_recv.at[d - 1], line_id(nz - d)).wait_recv()
        own = own + line_in[d - 1].astype(f32)
    dk_ref[...] = (own[0] * scale).astype(bf16)
    dv_ref[...] = own[1].astype(bf16)

    for copy in xc + zc[1:] + list(pc.values()) + list(rc.values()) + [qc] + lc[1:]:
        copy.wait_send()


def local(query_rows, key_matrix, value_matrix, output_rows, out_grad, log_norm, span_order):
    f32, bf16 = jnp.float32, jnp.bfloat16
    t, heads, d = query_rows.shape
    nz = lax.axis_size("ctx") // 2
    rows = t * heads
    keys = nz * t
    flat = lambda a: a.reshape(-1, d)
    vm = pl.BlockSpec(memory_space=pltpu.VMEM)
    dma = lambda *s: pltpu.SemaphoreType.DMA(s)
    dq, dk, dv = pl.pallas_call(
        functools.partial(kernel, nz),
        out_shape=(jax.ShapeDtypeStruct((rows, d), bf16), jax.ShapeDtypeStruct((t, d), bf16),
                   jax.ShapeDtypeStruct((t, d), bf16)),
        in_specs=[pl.BlockSpec(memory_space=pltpu.SMEM)] + [vm] * 6,
        out_specs=(vm, vm, vm),
        scratch_shapes=[
            pltpu.VMEM((4, nz, 2, t, d), bf16),
            pltpu.VMEM((rows, d), bf16),
            pltpu.VMEM((rows, d), bf16),
            pltpu.VMEM((2, rows), f32),
            pltpu.VMEM((2, rows), f32),
            pltpu.VMEM((d, keys), bf16),
            pltpu.VMEM((2, keys, d), f32),
            pltpu.VMEM((2, keys, d), f32),
            pltpu.VMEM((d, rows), f32),
            pltpu.VMEM((d, rows), f32),
            pltpu.VMEM((rows, d), bf16),
            pltpu.VMEM((rows, d), bf16),
            pltpu.VMEM((3, nz, 2, t, d), bf16),
            pltpu.VMEM((3, nz, 2, t, d), bf16),
            pltpu.VMEM((nz - 1, 2, t, d), bf16),
            pltpu.VMEM((nz - 1, 2, t, d), bf16),
            dma(3), dma(3), dma(nz), dma(nz), dma(4, nz), dma(4, nz),
            pltpu.SemaphoreType.DMA, pltpu.SemaphoreType.DMA,
            dma(3), dma(3), dma(nz - 1), dma(nz - 1),
        ],
        compiler_params=pltpu.CompilerParams(
            collective_id=0, has_side_effects=True, vmem_limit_bytes=48 * 1024 * 1024),
    )(span_order, flat(query_rows), flat(key_matrix), flat(value_matrix), flat(output_rows),
      flat(out_grad), log_norm.reshape(1, rows))
    return dq.reshape(query_rows.shape), dk.reshape(key_matrix.shape), dv.reshape(value_matrix.shape)


def solution(mesh):
    three = P(("ctx", "head"), None, None)
    in_specs = (three, three, three, three, three, P(("ctx", "head"), None), P())
    out_specs = (three, three, three)
    return jax.shard_map(local, mesh=mesh, in_specs=in_specs, out_specs=out_specs, check_vma=False)
```

```python
import functools

import jax
import jax.numpy as jnp
from jax import lax
from jax.experimental import pallas as pl
from jax.experimental.pallas import tpu as pltpu
from jax.sharding import PartitionSpec as P

MESH = pl.DeviceIdType.MESH
LOG2E = 1.4426950408889634
BIG = 1e30


def dot(a, b, ca, cb):
    return lax.dot_general(a, b, (((ca,), (cb,)), ((), ())), preferred_element_type=jnp.float32)


def chunk_size(rows, keys):
    chunk = 1536 if keys <= 512 else 128
    while rows % chunk:
        chunk //= 2
    return chunk


def kernel(nz, span_ref, q_hbm, k_ref, v_ref, o_hbm, do_hbm, lse_hbm, dq_ref, dk_ref, dv_ref,
           q_ref, o_ref, do_ref, lse_ref, in_sem, kv, pq, pdo, stats, pstats, kt, acc, acc0, dqt, dqt_p, dq_out, dq_in,
           part_out, part_in, line_out, line_in,
           x_send, x_recv, z_send, z_recv, p_send, p_recv, q_send, q_recv,
           r_send, r_recv, l_send, l_recv):
    f32, bf16 = jnp.float32, jnp.bfloat16
    t = k_ref.shape[0]
    head_size = k_ref.shape[1]
    rows = q_ref.shape[0]
    heads = rows // t
    keys = nz * t
    scale = head_size ** -0.5
    c = lax.axis_index("ctx")
    h = lax.axis_index("head")
    core = lax.rem(h, 2)
    x = lax.div(h, 2)
    y = lax.rem(c, 2)
    z = lax.div(c, 2)

    partner = {"ctx": c, "head": x * 2 + (1 - core)}

    def plane(q):
        xx = 1 - x if q % 2 else x
        yy = 1 - y if q // 2 else y
        return xx, yy

    def plane_id(q):
        xx, yy = plane(q)
        return {"ctx": z * 2 + yy, "head": xx * 2 + core}

    def line_id(d):
        return {"ctx": lax.rem(z + d, nz) * 2 + y, "head": h}

    loads = [pltpu.make_async_copy(src, dst, in_sem.at[i]) for i, (src, dst) in enumerate((
        (k_ref, kv.at[0, 0, 0]), (v_ref, kv.at[0, 0, 1]), (do_hbm, do_ref), (o_hbm, o_ref),
        (lse_hbm, lse_ref), (q_hbm, q_ref)))]
    for load in loads:
        load.start()
    barrier = pltpu.get_barrier_semaphore()
    peers = [partner] + [plane_id(q) for q in (1, 2, 3)] + [line_id(d) for d in range(1, nz)]
    for peer in peers:
        pl.semaphore_signal(barrier, inc=1, device_id=peer, device_id_type=MESH)

    loads[0].wait()
    loads[1].wait()
    pl.semaphore_wait(barrier, len(peers))

    def remote(src, dst, ss, rs, dev):
        return pltpu.make_async_remote_copy(
            src_ref=src, dst_ref=dst, send_sem=ss, recv_sem=rs, device_id=dev, device_id_type=MESH)

    zc = [None] + [remote(kv.at[0, 0], kv.at[0, nz - d], z_send.at[d], z_recv.at[nz - d], line_id(d))
                   for d in range(1, nz)]
    pc = {(q, d): remote(kv.at[0, d], kv.at[q, d], p_send.at[q, d], p_recv.at[q, d], plane_id(q))
          for q in (1, 2) for d in range(nz)}
    for d in range(nz):
        for half in range(2):
            pc[3 + half, d] = remote(
                kv.at[1 + half, d, half], kv.at[3, d, half], p_send.at[3 + half, d],
                p_recv.at[3 + half, d], plane_id(2 - half))
    xc = [remote(q_hbm, pq, x_send.at[0], x_recv.at[0], partner),
          remote(do_hbm, pdo, x_send.at[1], x_recv.at[1], partner),
          remote(stats, pstats, x_send.at[2], x_recv.at[2], partner)]
    for d in range(1, nz):
        zc[d].start()
    for q in (1, 2):
        pc[q, 0].start()
    xc[0].start()
    xc[1].start()
    loads[2].wait()
    loads[3].wait()
    prod = o_ref[...].astype(f32) * do_ref[...].astype(f32)
    prod_hi = prod.astype(bf16)
    prod_lo = (prod - prod_hi.astype(f32)).astype(bf16)
    ones = jnp.ones((8, head_size), bf16)
    delta = dot(ones, prod_hi, 1, 1) + dot(ones, prod_lo, 1, 1)
    loads[4].wait()
    rest = lse_ref[...]
    pick = (lax.div(lax.broadcasted_iota(jnp.int32, (t, rows), 1), heads)
            == lax.broadcasted_iota(jnp.int32, (t, rows), 0)).astype(f32).astype(bf16)
    spread = jnp.zeros((heads, rows), f32)
    for _ in range(3):
        piece = rest.astype(bf16)
        rest = rest - piece.astype(f32)
        spread = spread + dot(piece, pick, 1, 0)
    mine = (lax.rem(lax.broadcasted_iota(jnp.int32, (heads, rows), 1), heads)
            == lax.broadcasted_iota(jnp.int32, (heads, rows), 0))
    stats[0:1, :] = jnp.sum(jnp.where(mine, spread, 0.0), axis=0, keepdims=True) * LOG2E
    stats[1:2, :] = delta[0:1, :]
    xc[2].start()
    loads[5].wait()


    def z_arrival(d):
        return remote(kv.at[0, 0], kv.at[0, d], z_send.at[nz - d], z_recv.at[d], line_id(nz - d))

    for d in sorted(range(1, nz), key=lambda d: min(d, nz - d)):
        z_arrival(d).wait_recv()
        for q in (1, 2):
            pc[q, d].start()

    own_span = c * (lax.axis_size("head") // 2) + x
    own_place = span_ref[own_span]
    chunk = chunk_size(rows, keys)

    def prepare(q):
        block = kv[q, :, 0].reshape(keys, head_size)
        kt[...] = block.astype(f32).T.astype(bf16)

    def work(q, row_q, row_do, row_stats, row_core, dq_acc, first, total, total_first):
        xx, yy = plane(q)
        lifts = []
        for d in range(nz):
            zz = lax.rem(z + d, nz)
            place = span_ref[(zz * 2 + yy) * (lax.axis_size("head") // 2) + xx]
            lifts.append(jnp.where(place > own_place, jnp.float32(BIG), jnp.float32(0.0)))
        if total_first:
            total[...] = jnp.zeros(total.shape, f32)

        def body(i, carry):
            low = pl.multiple_of(i * chunk, chunk)
            at = pl.ds(low, chunk)
            qs = row_q[at, :]
            gs = row_do[at, :]
            lse = row_stats[0:1, at]
            delt = row_stats[1:2, at]
            kb = kv[q, :, 0].reshape(keys, head_size)
            vb = kv[q, :, 1].reshape(keys, head_size)
            s = dot(kb, qs, 1, 1)
            dp = dot(vb, gs, 1, 1)
            ps, dss = [], []
            for d in range(nz):
                part = slice(d * t, (d + 1) * t)
                e = s[part] * (scale * LOG2E) - (lse + lifts[d])
                if q == 0 and d == 0:
                    key_at = lax.broadcasted_iota(jnp.int32, (t, chunk), 0) + core * t
                    row_at = lax.broadcasted_iota(jnp.int32, (t, chunk), 1) + low
                    row_at = lax.div(row_at, heads) + row_core * t
                    e = jnp.where(key_at <= row_at, e, -BIG)
                p = jnp.exp2(e)
                ps.append(p.astype(bf16))
                dss.append((p * (dp[part] - delt)).astype(bf16))
            p = jnp.concatenate(ps, axis=0)
            ds = jnp.concatenate(dss, axis=0)
            total[0] += dot(ds, qs, 1, 0)
            total[1] += dot(p, gs, 1, 0)
            dqt = dot(kt[...], ds, 1, 0)
            if first:
                dq_acc[:, at] = dqt
            else:
                dq_acc[:, at] += dqt
            return carry

        lax.fori_loop(0, rows // chunk, body, 0)

    for copy in xc:
        copy.wait_recv()
    prepare(0)
    work(0, pq, pdo, pstats, 1 - core, dqt_p, True, acc0, True)
    for d in [0] + sorted(range(1, nz), key=lambda d: min(d, nz - d)):
        for q in (1, 2):
            pc[q, d].wait_recv()
            pc[q + 2, d].start()
    rc = {}
    for q in (1, 2, 3):
        if q == 3:
            for d in range(nz):
                pc[3, d].wait_recv()
                pc[4, d].wait_recv()
        prepare(q)
        work(q, pq, pdo, pstats, 1 - core, dqt_p, False, acc, True)
        work(q, q_ref, do_ref, stats, core, dqt, q == 1, acc, False)
        for d in range(nz):
            part_out[q - 1, d] = acc[:, d * t:(d + 1) * t, :].astype(bf16)
        rc[q] = remote(part_out.at[q - 1], part_in.at[q - 1], r_send.at[q - 1], r_recv.at[q - 1], plane_id(q))
        rc[q].start()
    dq_out[...] = dqt_p[...].T.astype(bf16)
    qc = remote(dq_out, dq_in, q_send, q_recv, partner)
    qc.start()
    prepare(0)
    work(0, q_ref, do_ref, stats, core, dqt, False, acc0, False)
    for q in (1, 2, 3):
        rc[q].wait_recv()

    def plane_sum(d):
        value = acc0[:, d * t:(d + 1) * t, :]
        for q in (1, 2, 3):
            value = value + part_in[q - 1, d].astype(f32)
        return value

    lc = [None]
    for d in range(1, nz):
        line_out[d - 1] = plane_sum(d).astype(bf16)
        lc.append(remote(line_out.at[d - 1], line_in.at[nz - d - 1], l_send.at[d - 1],
                         l_recv.at[nz - d - 1], line_id(d)))
        lc[d].start()
    own = plane_sum(0)
    qc.wait_recv()
    dq_ref[...] = ((dqt[...].T + dq_in[...].astype(f32)) * scale).astype(bf16)
    for d in range(1, nz):
        remote(line_out.at[nz - d - 1], line_in.at[d - 1], l_send.at[nz - d - 1],
               l_recv.at[d - 1], line_id(nz - d)).wait_recv()
        own = own + line_in[d - 1].astype(f32)
    dk_ref[...] = (own[0] * scale).astype(bf16)
    dv_ref[...] = own[1].astype(bf16)

    for copy in xc + zc[1:] + list(pc.values()) + list(rc.values()) + [qc] + lc[1:]:
        copy.wait_send()


def local(query_rows, key_matrix, value_matrix, output_rows, out_grad, log_norm, span_order):
    f32, bf16 = jnp.float32, jnp.bfloat16
    t, heads, d = query_rows.shape
    nz = lax.axis_size("ctx") // 2
    rows = t * heads
    keys = nz * t
    flat = lambda a: a.reshape(-1, d)
    vm = pl.BlockSpec(memory_space=pltpu.VMEM)
    hbm = pl.BlockSpec(memory_space=pltpu.HBM)
    dma = lambda *s: pltpu.SemaphoreType.DMA(s)
    dq, dk, dv = pl.pallas_call(
        functools.partial(kernel, nz),
        out_shape=(jax.ShapeDtypeStruct((rows, d), bf16), jax.ShapeDtypeStruct((t, d), bf16),
                   jax.ShapeDtypeStruct((t, d), bf16)),
        in_specs=[pl.BlockSpec(memory_space=pltpu.SMEM)] + [hbm] * 6,
        out_specs=(vm, vm, vm),
        scratch_shapes=[
            pltpu.VMEM((rows, d), bf16),
            pltpu.VMEM((rows, d), bf16),
            pltpu.VMEM((rows, d), bf16),
            pltpu.VMEM((heads, t), f32),
            dma(6),
            pltpu.VMEM((4, nz, 2, t, d), bf16),
            pltpu.VMEM((rows, d), bf16),
            pltpu.VMEM((rows, d), bf16),
            pltpu.VMEM((2, rows), f32),
            pltpu.VMEM((2, rows), f32),
            pltpu.VMEM((d, keys), bf16),
            pltpu.VMEM((2, keys, d), f32),
            pltpu.VMEM((2, keys, d), f32),
            pltpu.VMEM((d, rows), f32),
            pltpu.VMEM((d, rows), f32),
            pltpu.VMEM((rows, d), bf16),
            pltpu.VMEM((rows, d), bf16),
            pltpu.VMEM((3, nz, 2, t, d), bf16),
            pltpu.VMEM((3, nz, 2, t, d), bf16),
            pltpu.VMEM((nz - 1, 2, t, d), bf16),
            pltpu.VMEM((nz - 1, 2, t, d), bf16),
            dma(3), dma(3), dma(nz), dma(nz), dma(5, nz), dma(5, nz),
            pltpu.SemaphoreType.DMA, pltpu.SemaphoreType.DMA,
            dma(3), dma(3), dma(nz - 1), dma(nz - 1),
        ],
        compiler_params=pltpu.CompilerParams(
            collective_id=0, has_side_effects=True, vmem_limit_bytes=63 * 1024 * 1024 + 512 * 1024),
    )(span_order, flat(query_rows), flat(key_matrix), flat(value_matrix), flat(output_rows),
      flat(out_grad), log_norm.T)
    return dq.reshape(query_rows.shape), dk.reshape(key_matrix.shape), dv.reshape(value_matrix.shape)


def solution(mesh):
    three = P(("ctx", "head"), None, None)
    in_specs = (three, three, three, three, three, P(("ctx", "head"), None), P())
    out_specs = (three, three, three)
    return jax.shard_map(local, mesh=mesh, in_specs=in_specs, out_specs=out_specs, check_vma=False)
```

```python
import functools

import jax
import jax.numpy as jnp
from jax import lax
from jax.experimental import pallas as pl
from jax.experimental.pallas import tpu as pltpu
from jax.sharding import PartitionSpec as P

MESH = pl.DeviceIdType.MESH
LOG2E = 1.4426950408889634
BIG = 1e30


def dot(a, b, ca, cb):
    return lax.dot_general(a, b, (((ca,), (cb,)), ((), ())), preferred_element_type=jnp.float32)


def chunk_size(rows, keys):
    chunk = 1536 if keys <= 512 else 128
    while rows % chunk:
        chunk //= 2
    return chunk


def kernel(nz, span_ref, q_hbm, k_ref, v_ref, o_hbm, do_hbm, lse_hbm, dq_ref, dk_ref, dv_ref,
           q_ref, o_ref, do_ref, lse_ref, in_sem, kv, pq, pdo, stats, pstats, kt, acc, acc0, dqt, dqt_p, dq_out, dq_in,
           part_out, part_in, line_out, line_in,
           x_send, x_recv, z_send, z_recv, p_send, p_recv, q_send, q_recv,
           r_send, r_recv, l_send, l_recv):
    f32, bf16 = jnp.float32, jnp.bfloat16
    t = k_ref.shape[0]
    head_size = k_ref.shape[1]
    rows = q_ref.shape[0]
    heads = rows // t
    keys = nz * t
    scale = head_size ** -0.5
    c = lax.axis_index("ctx")
    h = lax.axis_index("head")
    core = lax.rem(h, 2)
    x = lax.div(h, 2)
    y = lax.rem(c, 2)
    z = lax.div(c, 2)

    partner = {"ctx": c, "head": x * 2 + (1 - core)}

    def plane(q):
        xx = 1 - x if q % 2 else x
        yy = 1 - y if q // 2 else y
        return xx, yy

    def plane_id(q):
        xx, yy = plane(q)
        return {"ctx": z * 2 + yy, "head": xx * 2 + core}

    def line_id(d):
        return {"ctx": lax.rem(z + d, nz) * 2 + y, "head": h}

    loads = [pltpu.make_async_copy(src, dst, in_sem.at[i]) for i, (src, dst) in enumerate((
        (k_ref, kv.at[0, 0, 0]), (v_ref, kv.at[0, 0, 1]), (do_hbm, do_ref), (o_hbm, o_ref),
        (lse_hbm, lse_ref), (q_hbm, q_ref)))]
    for load in loads:
        load.start()
    barrier = pltpu.get_barrier_semaphore()
    peers = [partner] + [plane_id(q) for q in (1, 2, 3)] + [line_id(d) for d in range(1, nz)]
    for peer in peers:
        pl.semaphore_signal(barrier, inc=1, device_id=peer, device_id_type=MESH)

    loads[0].wait()
    loads[1].wait()
    pl.semaphore_wait(barrier, len(peers))

    def remote(src, dst, ss, rs, dev):
        return pltpu.make_async_remote_copy(
            src_ref=src, dst_ref=dst, send_sem=ss, recv_sem=rs, device_id=dev, device_id_type=MESH)

    zc = [None] + [remote(kv.at[0, 0], kv.at[0, nz - d], z_send.at[d], z_recv.at[nz - d], line_id(d))
                   for d in range(1, nz)]
    pc = {(q, d): remote(kv.at[0, d], kv.at[q, d], p_send.at[q, d], p_recv.at[q, d], plane_id(q))
          for q in (1, 2) for d in range(nz)}
    for d in range(nz):
        for half in range(2):
            pc[3 + half, d] = remote(
                kv.at[1 + half, d, half], kv.at[3, d, half], p_send.at[3 + half, d],
                p_recv.at[3 + half, d], plane_id(2 - half))
    xc = [remote(q_hbm, pq, x_send.at[0], x_recv.at[0], partner),
          remote(do_hbm, pdo, x_send.at[1], x_recv.at[1], partner),
          remote(stats, pstats, x_send.at[2], x_recv.at[2], partner)]
    for d in range(1, nz):
        zc[d].start()
    for q in (1, 2):
        pc[q, 0].start()
    xc[0].start()
    xc[1].start()
    loads[2].wait()
    loads[3].wait()
    prod = o_ref[...].astype(f32) * do_ref[...].astype(f32)
    prod_hi = prod.astype(bf16)
    prod_lo = (prod - prod_hi.astype(f32)).astype(bf16)
    ones = jnp.ones((8, head_size), bf16)
    delta = dot(ones, prod_hi, 1, 1) + dot(ones, prod_lo, 1, 1)
    loads[4].wait()
    rest = lse_ref[...]
    pick = (lax.div(lax.broadcasted_iota(jnp.int32, (t, rows), 1), heads)
            == lax.broadcasted_iota(jnp.int32, (t, rows), 0)).astype(f32).astype(bf16)
    spread = jnp.zeros((heads, rows), f32)
    for _ in range(3):
        piece = rest.astype(bf16)
        rest = rest - piece.astype(f32)
        spread = spread + dot(piece, pick, 1, 0)
    mine = (lax.rem(lax.broadcasted_iota(jnp.int32, (heads, rows), 1), heads)
            == lax.broadcasted_iota(jnp.int32, (heads, rows), 0))
    stats[0:1, :] = jnp.sum(jnp.where(mine, spread, 0.0), axis=0, keepdims=True) * LOG2E
    stats[1:2, :] = delta[0:1, :]
    xc[2].start()
    loads[5].wait()


    def z_arrival(d):
        return remote(kv.at[0, 0], kv.at[0, d], z_send.at[nz - d], z_recv.at[d], line_id(nz - d))

    for d in sorted(range(1, nz), key=lambda d: min(d, nz - d)):
        z_arrival(d).wait_recv()
        for q in (1, 2):
            pc[q, d].start()

    own_span = c * (lax.axis_size("head") // 2) + x
    own_place = span_ref[own_span]
    chunk = chunk_size(rows, keys)

    def prepare(q):
        block = kv[q, :, 0].reshape(keys, head_size)
        kt[...] = block.astype(f32).T.astype(bf16)

    def work(q, row_q, row_do, row_stats, row_core, dq_acc, first, total, total_first):
        xx, yy = plane(q)
        lifts = []
        for d in range(nz):
            zz = lax.rem(z + d, nz)
            place = span_ref[(zz * 2 + yy) * (lax.axis_size("head") // 2) + xx]
            lifts.append(jnp.where(place > own_place, jnp.float32(BIG), jnp.float32(0.0)))
        if total_first:
            total[...] = jnp.zeros(total.shape, f32)

        def body(i, carry):
            low = pl.multiple_of(i * chunk, chunk)
            at = pl.ds(low, chunk)
            qs = row_q[at, :]
            gs = row_do[at, :]
            lse = row_stats[0:1, at]
            delt = row_stats[1:2, at]
            kb = kv[q, :, 0].reshape(keys, head_size)
            vb = kv[q, :, 1].reshape(keys, head_size)
            s = dot(kb, qs, 1, 1)
            dp = dot(vb, gs, 1, 1)
            ps, dss = [], []
            for d in range(nz):
                part = slice(d * t, (d + 1) * t)
                e = s[part] * (scale * LOG2E) - (lse + lifts[d])
                if q == 0 and d == 0:
                    key_at = lax.broadcasted_iota(jnp.int32, (t, chunk), 0) + core * t
                    row_at = lax.broadcasted_iota(jnp.int32, (t, chunk), 1) + low
                    row_at = lax.div(row_at, heads) + row_core * t
                    e = jnp.where(key_at <= row_at, e, -BIG)
                p = jnp.exp2(e)
                ps.append(p.astype(bf16))
                dss.append((p * (dp[part] - delt)).astype(bf16))
            p = jnp.concatenate(ps, axis=0)
            ds = jnp.concatenate(dss, axis=0)
            total[0] += dot(ds, qs, 1, 0)
            total[1] += dot(p, gs, 1, 0)
            dqt = dot(kt[...], ds, 1, 0)
            if first:
                dq_acc[:, at] = dqt
            else:
                dq_acc[:, at] += dqt
            return carry

        lax.fori_loop(0, rows // chunk, body, 0)

    for copy in xc:
        copy.wait_recv()
    prepare(0)
    work(0, pq, pdo, pstats, 1 - core, dqt_p, True, acc0, True)
    for d in [0] + sorted(range(1, nz), key=lambda d: min(d, nz - d)):
        for q in (1, 2):
            pc[q, d].wait_recv()
            pc[q + 2, d].start()
    rc = {}
    far_first = sorted(range(nz), key=lambda d: -min(d, nz - d))
    for q in (1, 2, 3):
        if q == 3:
            for d in range(nz):
                pc[3, d].wait_recv()
                pc[4, d].wait_recv()
        prepare(q)
        work(q, pq, pdo, pstats, 1 - core, dqt_p, False, acc, True)
        work(q, q_ref, do_ref, stats, core, dqt, q == 1, acc, False)
        for d in far_first:
            part_out[q - 1, d] = acc[:, d * t:(d + 1) * t, :].astype(bf16)
            rc[q, d] = remote(part_out.at[q - 1, d], part_in.at[q - 1, d], r_send.at[q - 1, d],
                              r_recv.at[q - 1, d], plane_id(q))
            rc[q, d].start()
    dq_out[...] = dqt_p[...].T.astype(bf16)
    qc = remote(dq_out, dq_in, q_send, q_recv, partner)
    qc.start()
    prepare(0)
    work(0, q_ref, do_ref, stats, core, dqt, False, acc0, False)

    def plane_sum(d):
        value = acc0[:, d * t:(d + 1) * t, :]
        for q in (1, 2, 3):
            rc[q, d].wait_recv()
            value = value + part_in[q - 1, d].astype(f32)
        return value

    lc = {}
    for d in far_first[:-1]:
        line_out[d - 1] = plane_sum(d).astype(bf16)
        lc[d] = remote(line_out.at[d - 1], line_in.at[nz - d - 1], l_send.at[d - 1],
                       l_recv.at[nz - d - 1], line_id(d))
        lc[d].start()
    own = plane_sum(0)
    qc.wait_recv()
    dq_ref[...] = ((dqt[...].T + dq_in[...].astype(f32)) * scale).astype(bf16)
    for d in range(1, nz):
        remote(line_out.at[nz - d - 1], line_in.at[d - 1], l_send.at[nz - d - 1],
               l_recv.at[d - 1], line_id(nz - d)).wait_recv()
        own = own + line_in[d - 1].astype(f32)
    dk_ref[...] = (own[0] * scale).astype(bf16)
    dv_ref[...] = own[1].astype(bf16)

    for copy in xc + zc[1:] + list(pc.values()) + list(rc.values()) + [qc] + list(lc.values()):
        copy.wait_send()


def local(query_rows, key_matrix, value_matrix, output_rows, out_grad, log_norm, span_order):
    f32, bf16 = jnp.float32, jnp.bfloat16
    t, heads, d = query_rows.shape
    nz = lax.axis_size("ctx") // 2
    rows = t * heads
    keys = nz * t
    flat = lambda a: a.reshape(-1, d)
    vm = pl.BlockSpec(memory_space=pltpu.VMEM)
    hbm = pl.BlockSpec(memory_space=pltpu.HBM)
    dma = lambda *s: pltpu.SemaphoreType.DMA(s)
    dq, dk, dv = pl.pallas_call(
        functools.partial(kernel, nz),
        out_shape=(jax.ShapeDtypeStruct((rows, d), bf16), jax.ShapeDtypeStruct((t, d), bf16),
                   jax.ShapeDtypeStruct((t, d), bf16)),
        in_specs=[pl.BlockSpec(memory_space=pltpu.SMEM)] + [hbm] * 6,
        out_specs=(vm, vm, vm),
        scratch_shapes=[
            pltpu.VMEM((rows, d), bf16),
            pltpu.VMEM((rows, d), bf16),
            pltpu.VMEM((rows, d), bf16),
            pltpu.VMEM((heads, t), f32),
            dma(6),
            pltpu.VMEM((4, nz, 2, t, d), bf16),
            pltpu.VMEM((rows, d), bf16),
            pltpu.VMEM((rows, d), bf16),
            pltpu.VMEM((2, rows), f32),
            pltpu.VMEM((2, rows), f32),
            pltpu.VMEM((d, keys), bf16),
            pltpu.VMEM((2, keys, d), f32),
            pltpu.VMEM((2, keys, d), f32),
            pltpu.VMEM((d, rows), f32),
            pltpu.VMEM((d, rows), f32),
            pltpu.VMEM((rows, d), bf16),
            pltpu.VMEM((rows, d), bf16),
            pltpu.VMEM((3, nz, 2, t, d), bf16),
            pltpu.VMEM((3, nz, 2, t, d), bf16),
            pltpu.VMEM((nz - 1, 2, t, d), bf16),
            pltpu.VMEM((nz - 1, 2, t, d), bf16),
            dma(3), dma(3), dma(nz), dma(nz), dma(5, nz), dma(5, nz),
            pltpu.SemaphoreType.DMA, pltpu.SemaphoreType.DMA,
            dma(3, nz), dma(3, nz), dma(nz - 1), dma(nz - 1),
        ],
        compiler_params=pltpu.CompilerParams(
            collective_id=0, has_side_effects=True, vmem_limit_bytes=63 * 1024 * 1024 + 512 * 1024),
    )(span_order, flat(query_rows), flat(key_matrix), flat(value_matrix), flat(output_rows),
      flat(out_grad), log_norm.T)
    return dq.reshape(query_rows.shape), dk.reshape(key_matrix.shape), dv.reshape(value_matrix.shape)


def solution(mesh):
    three = P(("ctx", "head"), None, None)
    in_specs = (three, three, three, three, three, P(("ctx", "head"), None), P())
    out_specs = (three, three, three)
    return jax.shard_map(local, mesh=mesh, in_specs=in_specs, out_specs=out_specs, check_vma=False)
```
